32 devices in a mesh: groups: 2 (over x), context: 16 (over z, y, core).
Axes of the slice: x: 2, y: 2, z: 4, core: 2. Of those that a mesh axis runs over, the one named last changes fastest.
Arguments:
- grad_out: bfloat16 [4096, 8192], P(('groups', 'context')), parts along dimension 0, may hold values from -0.125 to 0.125
- saved: bfloat16 [4096, 8192], P(('groups', 'context')), parts along dimension 0, may hold values from -6 to 6
- block_route: int32 [32, 16], P('groups'), parts along dimension 0, may hold values from 0 to 15, each once within a row
Outputs:
- weight_grad: bfloat16 [16384, 8192], P(('groups', 'context')), parts along dimension 0
The draws below stay inside these ranges and needn't reach their ends.
There are 2 independent parts, one for each index of `groups`. The reference program is written for one: setup_inputs(seed, part) draws one part's arguments, and reference() takes and returns one part's arrays. A program takes and returns all parts, laid end to end along the dimension named above; each array names one. Nothing has to cross between parts.
Inputs may be any that keep to these rules, and one draw needn't show every extreme that they name: Each row of block_route is a permutation of 0 to 15.
All inputs are finite; a program needn't handle non-finite values.
Results may differ from the reference program's by a relative error of at most 0.001.
Values may be sent and summed in bfloat16 or wider, within the bound.
A program may use at most 128 MiB of HBM per device.

```python
import jax
import jax.numpy as jnp
from jax import lax

D = 8192
TOK_DEV = 128
H = 8192
TOKENS = 2048
BLOCK = 8
N_CONTEXT = 16


def block_scale(stream_key, dims, shards, least, high):
    loudness, own = 1.0, jax.random.fold_in(stream_key, 6)
    for axis_at, parts in shards:
        heights = jnp.exp(jax.random.uniform(jax.random.fold_in(own, axis_at), (parts,), jnp.float32, least / len(shards), high / len(shards)))
        loudness = loudness * jnp.repeat(heights, dims[axis_at] // parts).reshape([-1 if axis == axis_at else 1 for axis in range(len(dims))])
    return loudness


def scatter_about(key, dims, scale, bound, pieces=(), kind=jnp.bfloat16):
    gain = block_scale(key, dims, pieces, -0.22, 0.18) if pieces else 1.0
    drawn = jax.random.normal(key, dims, jnp.float32) * scale * gain
    return jnp.minimum(jnp.maximum(drawn, -bound), bound).astype(kind)


def setup_inputs(seed: int = 0, part: int = 0) -> dict:
    key_list = jax.random.split(jax.random.key(seed), 4)
    own_keys = jax.random.split(jax.random.fold_in(key_list[3], part), 4)
    grad_out = scatter_about(own_keys[0], (TOKENS, D), TOKENS ** -0.5, 0.125, ((0, 16),))
    saved = scatter_about(own_keys[1], (TOKENS, H), 1.0, 6.0, ((0, 16),))
    block_route = jax.vmap(lambda own: jax.random.permutation(own, N_CONTEXT))(jax.random.split(own_keys[2], N_CONTEXT)).reshape((N_CONTEXT, N_CONTEXT)).astype(jnp.int32)
    return dict(grad_out=grad_out, saved=saved, block_route=block_route)


def routed_order(block_route, devices, tok_rows, blocksize):
    sources = jnp.arange(devices, dtype=jnp.int32)
    starts = sources[None, :] * tok_rows + block_route.T.astype(jnp.int32) * blocksize
    offsets = jnp.arange(blocksize, dtype=jnp.int32)
    return (starts[:, :, None] + offsets[None, None, :]).reshape(-1).astype(jnp.int32)


def reference(grad_out, saved, block_route):
    positions = routed_order(block_route, N_CONTEXT, TOK_DEV, BLOCK)
    zig_grad = jnp.take(grad_out, positions, axis=0)
    product = lax.dot_general(saved, zig_grad, (((0,), (0,)), ((), ())), preferred_element_type=jnp.float32)
    return product.astype(jnp.bfloat16)
```

```python
import math

import jax
import jax.numpy as jnp
from jax import lax
from jax.sharding import PartitionSpec as P


def partner(array, axis, apart):
    return lax.ppermute(array, axis, [(i, i ^ 1 << apart) for i in range(lax.axis_size(axis))])


def routed_order(block_route, devices, tok_rows, blocksize):
    sources = jnp.arange(devices, dtype=jnp.int32)
    starts = sources[None, :] * tok_rows + block_route.T * blocksize
    offsets = jnp.arange(blocksize, dtype=jnp.int32)
    return (starts[:, :, None] + offsets[None, None, :]).reshape(-1)


def join_pair(mine, other, upper, axis_dim):
    lower_first = jnp.concatenate((mine, other), axis=axis_dim)
    upper_first = jnp.concatenate((other, mine), axis=axis_dim)
    return jnp.where(upper, upper_first, lower_first)


def grid_body(grad_out, saved, block_route):
    devices = lax.axis_size("context")
    side = math.isqrt(devices)
    levels = side.bit_length() - 1
    myself = lax.axis_index("context")
    tok_rows, width = grad_out.shape
    inner = saved.shape[1]
    blocksize = tok_rows // devices
    head_piece = inner // devices
    model_piece = width // devices
    head_cols, model_cols = (
        lax.all_to_all(saved, "context", split_axis=1, concat_axis=0, tiled=True),
        lax.all_to_all(grad_out, "context", split_axis=1, concat_axis=0, tiled=True),
    )
    model_cols = jnp.take(
        model_cols, routed_order(block_route, devices, tok_rows, blocksize), axis=0
    )
    for level in range(levels):
        other = partner(head_cols, "context", level)
        head_cols = join_pair(head_cols, other, myself >> level & 1 == 1, 1)
    for level in range(levels):
        other = partner(model_cols, "context", levels + level)
        model_cols = join_pair(model_cols, other, myself >> levels + level & 1 == 1, 1)
    product = lax.dot_general(
        head_cols, model_cols, (((0,), (0,)), ((), ())), preferred_element_type=jnp.float32
    )
    tile_cols = side * model_piece
    slots = product.astype(jnp.bfloat16).reshape(side, head_piece, tile_cols)
    for level in range(levels):
        upper = myself >> level & 1 == 1
        shaped = slots.reshape(side >> level + 1, 2, 1 << level, head_piece, tile_cols)
        outgoing_half = jnp.where(upper, shaped[:, 0], shaped[:, 1])
        incoming_half = partner(outgoing_half, "context", level)
        first_half = jnp.where(upper, incoming_half, shaped[:, 0])
        second_half = jnp.where(upper, shaped[:, 1], incoming_half)
        slots = jnp.stack((first_half, second_half), axis=1).reshape(side, head_piece, tile_cols)
    arranged = slots.reshape(side, head_piece, side, model_piece).transpose(1, 2, 0, 3)
    return arranged.reshape(head_piece, width)


def gather_body(grad_out, saved, block_route):
    devices = lax.axis_size("context")
    myself = lax.axis_index("context")
    tok_rows, width = grad_out.shape
    inner = saved.shape[1]
    blocksize = tok_rows // devices
    route = lax.dynamic_index_in_dim(block_route, myself, 0, keepdims=False)
    mine = jnp.take(grad_out.reshape(devices, blocksize, width), route, axis=0)
    grad = lax.all_gather(mine.reshape(tok_rows, width), "context", axis=0, tiled=True)
    head = lax.all_to_all(saved, "context", split_axis=1, concat_axis=0, tiled=True)
    head = head.reshape(devices, devices, blocksize, inner // devices).transpose(1, 0, 2, 3)
    head = head.reshape(devices * tok_rows, inner // devices)
    product = lax.dot_general(
        head, grad, (((0,), (0,)), ((), ())), preferred_element_type=jnp.float32
    )
    return product.astype(jnp.bfloat16)


def body(grad_out, saved, block_route):
    gathered = lax.axis_size("context") * grad_out.size * grad_out.dtype.itemsize
    if gathered <= 2 ** 25:
        return gather_body(grad_out, saved, block_route)
    return grid_body(grad_out, saved, block_route)


def solution(mesh):
    return jax.shard_map(
        body,
        mesh=mesh,
        in_specs=(
            P(("groups", "context"), None),
            P(("groups", "context"), None),
            P("groups", None),
        ),
        out_specs=P(("groups", "context"), None),
        check_vma=False,
    )
```

```python
import functools
import math

import jax
import jax.numpy as jnp
from jax import lax
from jax.experimental import pallas as pl
from jax.experimental.pallas import tpu as pltpu
from jax.sharding import PartitionSpec as P


def partner(array, axis, apart):
    return lax.ppermute(array, axis, [(i, i ^ 1 << apart) for i in range(lax.axis_size(axis))])


def routed_order(block_route, devices, tok_rows, blocksize):
    sources = jnp.arange(devices, dtype=jnp.int32)
    starts = sources[None, :] * tok_rows + block_route.T * blocksize
    offsets = jnp.arange(blocksize, dtype=jnp.int32)
    return (starts[:, :, None] + offsets[None, None, :]).reshape(-1)


def join_pair(mine, other, upper, axis_dim):
    lower_first = jnp.concatenate((mine, other), axis=axis_dim)
    upper_first = jnp.concatenate((other, mine), axis=axis_dim)
    return jnp.where(upper, upper_first, lower_first)


def grid_body(grad_out, saved, block_route):
    devices = lax.axis_size("context")
    side = math.isqrt(devices)
    levels = side.bit_length() - 1
    myself = lax.axis_index("context")
    tok_rows, width = grad_out.shape
    inner = saved.shape[1]
    blocksize = tok_rows // devices
    head_piece = inner // devices
    model_piece = width // devices
    head_cols, model_cols = (
        lax.all_to_all(saved, "context", split_axis=1, concat_axis=0, tiled=True),
        lax.all_to_all(grad_out, "context", split_axis=1, concat_axis=0, tiled=True),
    )
    model_cols = jnp.take(
        model_cols, routed_order(block_route, devices, tok_rows, blocksize), axis=0
    )
    for level in range(levels):
        other = partner(head_cols, "context", level)
        head_cols = join_pair(head_cols, other, myself >> level & 1 == 1, 1)
    for level in range(levels):
        other = partner(model_cols, "context", levels + level)
        model_cols = join_pair(model_cols, other, myself >> levels + level & 1 == 1, 1)
    product = lax.dot_general(
        head_cols, model_cols, (((0,), (0,)), ((), ())), preferred_element_type=jnp.float32
    )
    tile_cols = side * model_piece
    slots = product.astype(jnp.bfloat16).reshape(side, head_piece, tile_cols)
    for level in range(levels):
        upper = myself >> level & 1 == 1
        shaped = slots.reshape(side >> level + 1, 2, 1 << level, head_piece, tile_cols)
        outgoing_half = jnp.where(upper, shaped[:, 0], shaped[:, 1])
        incoming_half = partner(outgoing_half, "context", level)
        first_half = jnp.where(upper, incoming_half, shaped[:, 0])
        second_half = jnp.where(upper, shaped[:, 1], incoming_half)
        slots = jnp.stack((first_half, second_half), axis=1).reshape(side, head_piece, tile_cols)
    arranged = slots.reshape(side, head_piece, side, model_piece).transpose(1, 2, 0, 3)
    return arranged.reshape(head_piece, width)


PLANE = 4
DEPTH = 4
CHUNKS = 8


def fused_kernel(
    g_ref, s_ref, out_ref,
    gbuf, sbuf, st, gt, obuf,
    gp_send, gp_recv, g_local, gz_send, gz_recv,
    sz_send, sz_recv, s_local, sy_send, sy_recv, sc_send, sc_recv, sf_send, sf_recv,
    o_send, o_recv, o_local,
):
    me = lax.axis_index("context")
    z, p = me // PLANE, me % PLANE
    over_y = (p + 2) % PLANE
    core = p + 1 - 2 * (p % 2)
    tok, width = g_ref.shape
    features = s_ref.shape[1]
    quarter = width // PLANE
    head = features // DEPTH
    wide = quarter // CHUNKS
    rows = head // PLANE
    part = tok // DEPTH

    def at(zz, pp):
        return {"context": zz * PLANE + pp}

    def copy(src, dst, send, recv, device):
        return pltpu.make_async_remote_copy(
            src_ref=src, dst_ref=dst, send_sem=send, recv_sem=recv,
            device_id=device, device_id_type=pl.DeviceIdType.MESH,
        )

    barrier = pltpu.get_barrier_semaphore()
    for k in range(1, PLANE):
        pl.semaphore_signal(barrier, inc=1, device_id=at(z, (p + k) % PLANE), device_id_type=pl.DeviceIdType.MESH)
        pl.semaphore_signal(barrier, inc=1, device_id=at((z + k) % DEPTH, p), device_id_type=pl.DeviceIdType.MESH)
    pl.semaphore_wait(barrier, PLANE + DEPTH - 2)

    def s_rows(zz, pp):
        return sbuf.at[pl.ds(pl.multiple_of((zz * PLANE + pp) * tok, tok), tok), :]

    def s_cols(zz):
        return s_ref.at[:, pl.ds(pl.multiple_of(zz * head, head), head)]

    def s_line(k):
        other = (z + k) % DEPTH
        return copy(s_cols(other), s_rows(z, p), sz_send.at[k], sz_recv.at[k], at(other, p))

    def s_line_from(k):
        other = (z - k + DEPTH) % DEPTH
        return copy(s_cols(other), s_rows(other, p), sz_send.at[k], sz_recv.at[k], at(other, p))

    def s_own():
        return pltpu.make_async_copy(s_cols(z), s_rows(z, p), s_local.at[0])

    def source(k):
        return (z - k + DEPTH) % DEPTH

    def s_across(k, pp):
        src = s_cols(z) if k == 0 else s_rows(source(k), pp)
        return copy(src, s_rows(source(k), pp), sy_send.at[k], sy_recv.at[k], at(z, over_y))

    def s_core(k, pp):
        src = s_cols(z) if k == 0 else s_rows(source(k), pp)
        return copy(src, s_rows(source(k), pp), sc_send.at[k], sc_recv.at[k], at(z, core))

    def s_pass(k, pp):
        return copy(s_rows(source(k), pp), s_rows(source(k), pp), sf_send.at[k], sf_recv.at[k], at(z, core))

    def g_cols(pp, j):
        return g_ref.at[:, pl.ds(pl.multiple_of(pp * quarter + j * wide, wide), wide)]

    def g_rows(j, pp):
        return gbuf.at[j, z, pl.ds(pl.multiple_of(pp * tok, tok), tok), :]

    def g_plane(j, k):
        other = (p + k) % PLANE
        return copy(g_cols(other, j), g_rows(j, p), gp_send.at[j, k], gp_recv.at[j, k], at(z, other))

    def g_plane_from(j, k):
        other = (p - k + PLANE) % PLANE
        return copy(g_cols(other, j), g_rows(j, other), gp_send.at[j, k], gp_recv.at[j, k], at(z, other))

    def g_own(j):
        return pltpu.make_async_copy(g_cols(p, j), g_rows(j, p), g_local.at[j])

    def g_line(j, up, hop):
        src = z - hop if up else z + hop
        to = z + 1 if up else z - 1
        way = 0 if up else 1
        block = gbuf.at[j, src]
        return copy(block, block, gz_send.at[way, hop, j], gz_recv.at[way, hop, j], at(to, p))

    def g_line_from(j, up, hop):
        src = z - hop - 1 if up else z + hop + 1
        to = z - 1 if up else z + 1
        way = 0 if up else 1
        block = gbuf.at[j, src]
        return copy(block, block, gz_send.at[way, hop, j], gz_recv.at[way, hop, j], at(to, p))

    def sends(up, hop):
        return (z - hop >= 0) & (z < DEPTH - 1) if up else (z + hop < DEPTH) & (z > 0)

    def takes(up, hop):
        return z - hop - 1 >= 0 if up else z + hop + 1 < DEPTH

    def own_chunk(j):
        g_own(j).wait()
        for k in range(1, PLANE):
            g_plane_from(j, k).wait_recv()
        for up in (True, False):
            @pl.when(sends(up, 0))
            def _():
                g_line(j, up, 0).start()

    def take_chunk(j, hop):
        for up in (True, False):
            @pl.when(takes(up, hop))
            def _():
                g_line_from(j, up, hop).wait_recv()
            if hop + 1 < DEPTH - 1:
                @pl.when(sends(up, hop + 1))
                def _():
                    g_line(j, up, hop + 1).start()

    def o_piece(j, pp):
        return obuf.at[j, pl.ds(pl.multiple_of(pp * rows, rows), rows), :]

    def o_cols(pp, j):
        return out_ref.at[:, pl.ds(pl.multiple_of(pp * quarter + j * wide, wide), wide)]

    def o_to(j, k):
        other = (p + k) % PLANE
        return copy(o_piece(j, other), o_cols(p, j), o_send.at[j, k], o_recv.at[j, k], at(z, other))

    def o_from(j, k):
        other = (p - k + PLANE) % PLANE
        return copy(o_piece(j, other), o_cols(other, j), o_send.at[j, k], o_recv.at[j, k], at(z, other))

    def o_own(j):
        return pltpu.make_async_copy(o_piece(j, p), o_cols(p, j), o_local.at[j])

    def compute(j):
        def place(pair, carry):
            for zz in range(DEPTH):
                pieces = [
                    gbuf[j, zz, pl.ds(pl.multiple_of(pp * tok + pair * 16, 16), 16), :].astype(jnp.float32)
                    for pp in range(PLANE)
                ]
                for half in range(2):
                    joined = jnp.concatenate([x[half * 8:half * 8 + 8] for x in pieces], axis=0)
                    base = pl.multiple_of((pair * 2 + half) * tok + zz * part, part)
                    gt[pl.ds(base, part), :] = joined.astype(jnp.bfloat16)
            return carry

        lax.fori_loop(0, tok // 16, place, 0)

        def tile(m, carry):
            owner = (p + 1 + m) % PLANE
            base = pl.multiple_of(owner * rows, rows)
            acc = jnp.dot(st[pl.ds(base, rows), :], gt[...], preferred_element_type=jnp.float32)
            obuf[j, pl.ds(base, rows), :] = acc.astype(jnp.bfloat16)
            return carry

        lax.fori_loop(0, PLANE, tile, 0)
        for k in (2, 1, 3):
            o_to(j, k).start()
        o_own(j).start()

    s_own().start()
    g_own(0).start()
    for k in range(1, PLANE):
        g_plane(0, k).start()
    for k in range(1, DEPTH):
        s_line(k).start()

    def start_chunk(j, carry):
        g_own(j).start()
        for k in range(1, PLANE):
            g_plane(j, k).start()
        return carry

    lax.fori_loop(1, CHUNKS, start_chunk, 0)
    s_across(0, p).start()
    s_core(0, p).start()
    own_chunk(0)
    own_chunk(1)
    for k in (1, 3, 2):
        s_line_from(k).wait_recv()
        s_across(k, p).start()
        s_core(k, p).start()
    own_chunk(2)
    take_chunk(0, 0)
    own_chunk(3)
    take_chunk(1, 0)
    take_chunk(0, 1)
    for k in (0, 1, 3, 2):
        s_across(k, over_y).wait_recv()
        s_pass(k, over_y).start()
    s_own().wait()
    for k in range(DEPTH):
        s_core(k, core).wait_recv()
        s_pass(k, (core + 2) % PLANE).wait_recv()

    def turn(d, carry):
        base = pl.multiple_of(d * tok, tok)
        st[:, pl.ds(base, tok)] = sbuf[pl.ds(base, tok), :].T
        return carry

    lax.fori_loop(0, DEPTH * PLANE, turn, 0)

    def step(j, carry):
        @pl.when(j + 4 < CHUNKS)
        def _():
            own_chunk(j + 4)

        @pl.when(j + 2 < CHUNKS)
        def _():
            take_chunk(j + 2, 0)

        @pl.when(j + 1 < CHUNKS)
        def _():
            take_chunk(j + 1, 1)

        take_chunk(j, 2)
        compute(j)
        return carry

    lax.fori_loop(0, CHUNKS, step, 0)

    for k in range(1, DEPTH):
        s_line(k).wait_send()
    for k in range(DEPTH):
        s_across(k, p).wait_send()
        s_core(k, p).wait_send()
        s_pass(k, over_y).wait_send()

    def finish(j, carry):
        for k in range(1, PLANE):
            g_plane(j, k).wait_send()
        for up in (True, False):
            for hop in range(DEPTH - 1):
                @pl.when(sends(up, hop))
                def _():
                    g_line(j, up, hop).wait_send()
        for k in range(1, PLANE):
            o_to(j, k).wait_send()
            o_from(j, k).wait_recv()
        o_own(j).wait()
        return carry

    lax.fori_loop(0, CHUNKS, finish, 0)


def fused_body(grad_out, saved, block_route):
    devices = lax.axis_size("context")
    myself = lax.axis_index("context")
    tok, width = grad_out.shape
    features = saved.shape[1]
    block = tok // devices
    route = lax.dynamic_index_in_dim(block_route, myself, 0, keepdims=False)
    mine = jnp.take(grad_out.reshape(devices, block, width), route, axis=0, mode="clip")
    mine = mine.reshape(tok, width)
    tokens = tok * devices
    head, quarter = features // DEPTH, width // PLANE
    wide = quarter // CHUNKS
    dma = pltpu.SemaphoreType.DMA
    return pl.pallas_call(
        fused_kernel,
        out_shape=jax.ShapeDtypeStruct((features // devices, width), jnp.bfloat16),
        in_specs=[pl.BlockSpec(memory_space=pl.ANY)] * 2,
        out_specs=pl.BlockSpec(memory_space=pl.ANY),
        scratch_shapes=[
            pltpu.VMEM((CHUNKS, DEPTH, tok * PLANE, wide), jnp.bfloat16),
            pltpu.VMEM((tokens, head), jnp.bfloat16),
            pltpu.VMEM((head, tokens), jnp.bfloat16),
            pltpu.VMEM((tokens, wide), jnp.bfloat16),
            pltpu.VMEM((CHUNKS, head, wide), jnp.bfloat16),
            dma((CHUNKS, PLANE)), dma((CHUNKS, PLANE)), dma((CHUNKS,)),
            dma((2, DEPTH, CHUNKS)), dma((2, DEPTH, CHUNKS)),
            dma((DEPTH,)), dma((DEPTH,)), dma((1,)),
            dma((DEPTH,)), dma((DEPTH,)), dma((DEPTH,)), dma((DEPTH,)),
            dma((DEPTH,)), dma((DEPTH,)),
            dma((CHUNKS, PLANE)), dma((CHUNKS, PLANE)), dma((CHUNKS,)),
        ],
        compiler_params=pltpu.CompilerParams(
            collective_id=0, has_side_effects=True, vmem_limit_bytes=56 * 2 ** 20
        ),
        cost_estimate=pl.CostEstimate(
            flops=2 * head * quarter * tokens, bytes_accessed=2 ** 24, transcendentals=0
        ),
    )(mine, saved)


def body(grad_out, saved, block_route):
    devices = lax.axis_size("context")
    tok, width = grad_out.shape
    fits = devices == PLANE * DEPTH and tok == devices * 8
    if fits and width % (PLANE * CHUNKS * 128) == 0 and saved.shape[1] % (devices * 128) == 0:
        return fused_body(grad_out, saved, block_route)
    return grid_body(grad_out, saved, block_route)


def solution(mesh):
    return jax.shard_map(
        body,
        mesh=mesh,
        in_specs=(
            P(("groups", "context"), None),
            P(("groups", "context"), None),
            P("groups", None),
        ),
        out_specs=P(("groups", "context"), None),
        check_vma=False,
    )
```

```python
import functools
import math

import jax
import jax.numpy as jnp
from jax import lax
from jax.experimental import pallas as pl
from jax.experimental.pallas import tpu as pltpu
from jax.sharding import PartitionSpec as P


def partner(array, axis, apart):
    return lax.ppermute(array, axis, [(i, i ^ 1 << apart) for i in range(lax.axis_size(axis))])


def routed_order(block_route, devices, tok_rows, blocksize):
    sources = jnp.arange(devices, dtype=jnp.int32)
    starts = sources[None, :] * tok_rows + block_route.T * blocksize
    offsets = jnp.arange(blocksize, dtype=jnp.int32)
    return (starts[:, :, None] + offsets[None, None, :]).reshape(-1)


def join_pair(mine, other, upper, axis_dim):
    lower_first = jnp.concatenate((mine, other), axis=axis_dim)
    upper_first = jnp.concatenate((other, mine), axis=axis_dim)
    return jnp.where(upper, upper_first, lower_first)


def grid_body(grad_out, saved, block_route):
    devices = lax.axis_size("context")
    side = math.isqrt(devices)
    levels = side.bit_length() - 1
    myself = lax.axis_index("context")
    tok_rows, width = grad_out.shape
    inner = saved.shape[1]
    blocksize = tok_rows // devices
    head_piece = inner // devices
    model_piece = width // devices
    head_cols, model_cols = (
        lax.all_to_all(saved, "context", split_axis=1, concat_axis=0, tiled=True),
        lax.all_to_all(grad_out, "context", split_axis=1, concat_axis=0, tiled=True),
    )
    model_cols = jnp.take(
        model_cols, routed_order(block_route, devices, tok_rows, blocksize), axis=0
    )
    for level in range(levels):
        other = partner(head_cols, "context", level)
        head_cols = join_pair(head_cols, other, myself >> level & 1 == 1, 1)
    for level in range(levels):
        other = partner(model_cols, "context", levels + level)
        model_cols = join_pair(model_cols, other, myself >> levels + level & 1 == 1, 1)
    product = lax.dot_general(
        head_cols, model_cols, (((0,), (0,)), ((), ())), preferred_element_type=jnp.float32
    )
    tile_cols = side * model_piece
    slots = product.astype(jnp.bfloat16).reshape(side, head_piece, tile_cols)
    for level in range(levels):
        upper = myself >> level & 1 == 1
        shaped = slots.reshape(side >> level + 1, 2, 1 << level, head_piece, tile_cols)
        outgoing_half = jnp.where(upper, shaped[:, 0], shaped[:, 1])
        incoming_half = partner(outgoing_half, "context", level)
        first_half = jnp.where(upper, incoming_half, shaped[:, 0])
        second_half = jnp.where(upper, shaped[:, 1], incoming_half)
        slots = jnp.stack((first_half, second_half), axis=1).reshape(side, head_piece, tile_cols)
    arranged = slots.reshape(side, head_piece, side, model_piece).transpose(1, 2, 0, 3)
    return arranged.reshape(head_piece, width)


PLANE = 4
DEPTH = 4
CHUNKS = 16
GROUP = 2


def fused_kernel(
    g_ref, s_ref, out_ref,
    gbuf, sbuf, st, gt, obuf,
    gp_send, gp_recv, g_local, gz_send, gz_recv,
    sz_send, sz_recv, s_local, sy_send, sy_recv, sc_send, sc_recv, sf_send, sf_recv,
    o_send, o_recv, o_local,
):
    me = lax.axis_index("context")
    z, p = me // PLANE, me % PLANE
    over_y = (p + 2) % PLANE
    core = p + 1 - 2 * (p % 2)
    tok, width = g_ref.shape
    features = s_ref.shape[1]
    quarter = width // PLANE
    head = features // DEPTH
    wide = quarter // CHUNKS
    rows = head // PLANE
    part = tok // DEPTH
    near = 1 + 2 * (p % 2)
    far = PLANE - near

    def at(zz, pp):
        return {"context": zz * PLANE + pp}

    def copy(src, dst, send, recv, device):
        return pltpu.make_async_remote_copy(
            src_ref=src, dst_ref=dst, send_sem=send, recv_sem=recv,
            device_id=device, device_id_type=pl.DeviceIdType.MESH,
        )

    barrier = pltpu.get_barrier_semaphore()
    for k in range(1, PLANE):
        pl.semaphore_signal(barrier, inc=1, device_id=at(z, (p + k) % PLANE), device_id_type=pl.DeviceIdType.MESH)
        pl.semaphore_signal(barrier, inc=1, device_id=at((z + k) % DEPTH, p), device_id_type=pl.DeviceIdType.MESH)
    pl.semaphore_wait(barrier, PLANE + DEPTH - 2)

    def s_rows(zz, pp):
        return sbuf.at[pl.ds(pl.multiple_of((zz * PLANE + pp) * tok, tok), tok), :]

    def s_cols(zz):
        return s_ref.at[:, pl.ds(pl.multiple_of(zz * head, head), head)]

    def s_line(k):
        other = (z + k) % DEPTH
        return copy(s_cols(other), s_rows(z, p), sz_send.at[k], sz_recv.at[k], at(other, p))

    def s_line_from(k):
        other = (z - k + DEPTH) % DEPTH
        return copy(s_cols(other), s_rows(other, p), sz_send.at[k], sz_recv.at[k], at(other, p))

    def s_own():
        return pltpu.make_async_copy(s_cols(z), s_rows(z, p), s_local.at[0])

    def source(k):
        return (z - k + DEPTH) % DEPTH

    def s_across(k, pp):
        src = s_cols(z) if isinstance(k, int) and k == 0 else s_rows(source(k), pp)
        return copy(src, s_rows(source(k), pp), sy_send.at[k], sy_recv.at[k], at(z, over_y))

    def s_core(k, pp):
        src = s_cols(z) if isinstance(k, int) and k == 0 else s_rows(source(k), pp)
        return copy(src, s_rows(source(k), pp), sc_send.at[k], sc_recv.at[k], at(z, core))

    def s_pass(k, pp):
        return copy(s_rows(source(k), pp), s_rows(source(k), pp), sf_send.at[k], sf_recv.at[k], at(z, core))

    def g_cols(pp, j):
        return g_ref.at[:, pl.ds(pl.multiple_of(pp * quarter + j * wide, wide), wide)]

    def g_rows(j, pp):
        return gbuf.at[j, z, pl.ds(pl.multiple_of(pp * tok, tok), tok), :]

    def g_plane(j, k):
        other = (p + k) % PLANE
        return copy(g_cols(other, j), g_rows(j, p), gp_send.at[j, k], gp_recv.at[j, k], at(z, other))

    def g_plane_from(j, k):
        other = (p - k + PLANE) % PLANE
        return copy(g_cols(other, j), g_rows(j, other), gp_send.at[j, k], gp_recv.at[j, k], at(z, other))

    def g_own(j):
        return pltpu.make_async_copy(g_cols(p, j), g_rows(j, p), g_local.at[j])

    def g_line(j, up, hop):
        src = z - hop if up else z + hop
        to = z + 1 if up else z - 1
        way = 0 if up else 1
        block = gbuf.at[j, src]
        return copy(block, block, gz_send.at[way, hop, j], gz_recv.at[way, hop, j], at(to, p))

    def g_line_from(j, up, hop):
        src = z - hop - 1 if up else z + hop + 1
        to = z - 1 if up else z + 1
        way = 0 if up else 1
        block = gbuf.at[j, src]
        return copy(block, block, gz_send.at[way, hop, j], gz_recv.at[way, hop, j], at(to, p))

    def sends(up, hop):
        return (z - hop >= 0) & (z < DEPTH - 1) if up else (z + hop < DEPTH) & (z > 0)

    def takes(up, hop):
        return z - hop - 1 >= 0 if up else z + hop + 1 < DEPTH

    def own_chunk(j):
        g_own(j).wait()
        for k in range(1, PLANE):
            g_plane_from(j, k).wait_recv()
        for up in (True, False):
            @pl.when(sends(up, 0))
            def _():
                g_line(j, up, 0).start()

    def take_chunk(j, hop):
        for up in (True, False):
            @pl.when(takes(up, hop))
            def _():
                g_line_from(j, up, hop).wait_recv()
            if hop + 1 < DEPTH - 1:
                @pl.when(sends(up, hop + 1))
                def _():
                    g_line(j, up, hop + 1).start()

    def o_piece(j, pp):
        return obuf.at[j, pl.ds(pl.multiple_of(pp * rows, rows), rows), :]

    def o_cols(pp, j):
        return out_ref.at[:, pl.ds(pl.multiple_of(pp * quarter + j * wide, wide), wide)]

    def o_to(j, k):
        other = (p + k) % PLANE
        return copy(o_piece(j, other), o_cols(p, j), o_send.at[j, k], o_recv.at[j, k], at(z, other))

    def o_from(j, k):
        other = (p - k + PLANE) % PLANE
        return copy(o_piece(j, other), o_cols(other, j), o_send.at[j, k], o_recv.at[j, k], at(z, other))

    def o_own(j):
        return pltpu.make_async_copy(o_piece(j, p), o_cols(p, j), o_local.at[j])

    def compute(j):
        def place(pair, carry):
            for zz in range(DEPTH):
                pieces = [
                    gbuf[j, zz, pl.ds(pl.multiple_of(pp * tok + pair * 16, 16), 16), :].astype(jnp.float32)
                    for pp in range(PLANE)
                ]
                for half in range(2):
                    joined = jnp.concatenate([x[half * 8:half * 8 + 8] for x in pieces], axis=0)
                    base = pl.multiple_of((pair * 2 + half) * tok + zz * part, part)
                    gt[pl.ds(base, part), :] = joined.astype(jnp.bfloat16)
            return carry

        lax.fori_loop(0, tok // 16, place, 0)

        def tile(m, carry):
            k = jnp.where(m == 0, 2, jnp.where(m == 1, far, jnp.where(m == 2, near, 0)))
            base = pl.multiple_of(((p + k) % PLANE) * rows, rows)
            acc = jnp.dot(st[pl.ds(base, rows), :], gt[...], preferred_element_type=jnp.float32)
            obuf[j, pl.ds(base, rows), :] = acc.astype(jnp.bfloat16)

            @pl.when(m < PLANE - 1)
            def _():
                o_to(j, k).start()

            return carry

        lax.fori_loop(0, PLANE, tile, 0)
        o_own(j).start()

    def turn(zz, pp):
        base = pl.multiple_of((zz * PLANE + pp) * tok, tok)
        st[:, pl.ds(base, tok)] = sbuf[pl.ds(base, tok), :].T

    def spread(k):
        s_line_from(k).wait_recv()
        s_across(k, p).start()
        s_core(k, p).start()

    def collect(k):
        s_across(k, over_y).wait_recv()
        s_pass(k, over_y).start()
        turn(source(k), p)
        turn(source(k), over_y)

    first = jnp.where(z < DEPTH // 2, 3, 1)
    second = jnp.where((z == 0) | (z == DEPTH - 1), 2, jnp.where(z == 1, 1, 3))
    third = 6 - first - second

    def start_chunk(j):
        g_own(j).start()
        for k in range(1, PLANE):
            g_plane(j, k).start()

    ahead = jnp.where(z == 0, 3, jnp.where(z == DEPTH - 1, 1, 2))
    then = jnp.where(z == 1, 3, jnp.where(z == 2, 1, 2))
    for k in (ahead, then, 6 - ahead - then):
        s_line(k).start()
    start_chunk(0)
    s_own().start()
    for j in range(1, GROUP):
        start_chunk(j)
    s_across(0, p).start()
    s_core(0, p).start()
    for j in range(GROUP, 3 * GROUP):
        start_chunk(j)

    def own_group(i):
        for j in range(i * GROUP, i * GROUP + GROUP):
            own_chunk(j)

    def take_group(i, hop):
        for j in range(i * GROUP, i * GROUP + GROUP):
            take_chunk(j, hop)

    own_group(0)
    spread(third)
    own_group(1)
    spread(second)
    spread(first)

    def start_rest(j, carry):
        start_chunk(j)
        return carry

    lax.fori_loop(3 * GROUP, CHUNKS, start_rest, 0)

    take_group(0, 0)
    own_group(2)
    s_own().wait()
    collect(0)
    take_group(1, 0)
    collect(first)
    take_group(0, 1)
    collect(second)
    collect(third)

    def gather(k, carry):
        s_core(k, core).wait_recv()
        s_pass(k, (core + 2) % PLANE).wait_recv()
        turn(source(k), core)
        turn(source(k), (core + 2) % PLANE)
        return carry

    lax.fori_loop(0, DEPTH, gather, 0)

    def step(j, carry):
        @pl.when((j + 3 >= 3 * GROUP) & (j + 3 < CHUNKS))
        def _():
            own_chunk(j + 3)

        @pl.when((j + 2 >= 2 * GROUP) & (j + 2 < CHUNKS))
        def _():
            take_chunk(j + 2, 0)

        @pl.when((j + 1 >= GROUP) & (j + 1 < CHUNKS))
        def _():
            take_chunk(j + 1, 1)

        take_chunk(j, 2)
        compute(j)
        return carry

    lax.fori_loop(0, CHUNKS, step, 0)

    for k in range(1, DEPTH):
        s_line(k).wait_send()
    for k in range(DEPTH):
        s_across(k, p).wait_send()
        s_core(k, p).wait_send()
        s_pass(k, over_y).wait_send()

    def finish(j, carry):
        for k in range(1, PLANE):
            g_plane(j, k).wait_send()
        for up in (True, False):
            for hop in range(DEPTH - 1):
                @pl.when(sends(up, hop))
                def _():
                    g_line(j, up, hop).wait_send()
        for k in range(1, PLANE):
            o_to(j, k).wait_send()
            o_from(j, k).wait_recv()
        o_own(j).wait()
        return carry

    lax.fori_loop(0, CHUNKS, finish, 0)


def fused_body(grad_out, saved, block_route):
    devices = lax.axis_size("context")
    myself = lax.axis_index("context")
    tok, width = grad_out.shape
    features = saved.shape[1]
    block = tok // devices
    route = lax.dynamic_index_in_dim(block_route, myself, 0, keepdims=False)
    mine = jnp.take(grad_out.reshape(devices, block, width), route, axis=0, mode="clip")
    mine = mine.reshape(tok, width)
    tokens = tok * devices
    head, quarter = features // DEPTH, width // PLANE
    wide = quarter // CHUNKS
    dma = pltpu.SemaphoreType.DMA
    return pl.pallas_call(
        fused_kernel,
        out_shape=jax.ShapeDtypeStruct((features // devices, width), jnp.bfloat16),
        in_specs=[pl.BlockSpec(memory_space=pl.ANY)] * 2,
        out_specs=pl.BlockSpec(memory_space=pl.ANY),
        scratch_shapes=[
            pltpu.VMEM((CHUNKS, DEPTH, tok * PLANE, wide), jnp.bfloat16),
            pltpu.VMEM((tokens, head), jnp.bfloat16),
            pltpu.VMEM((head, tokens), jnp.bfloat16),
            pltpu.VMEM((tokens, wide), jnp.bfloat16),
            pltpu.VMEM((CHUNKS, head, wide), jnp.bfloat16),
            dma((CHUNKS, PLANE)), dma((CHUNKS, PLANE)), dma((CHUNKS,)),
            dma((2, DEPTH, CHUNKS)), dma((2, DEPTH, CHUNKS)),
            dma((DEPTH,)), dma((DEPTH,)), dma((1,)),
            dma((DEPTH,)), dma((DEPTH,)), dma((DEPTH,)), dma((DEPTH,)),
            dma((DEPTH,)), dma((DEPTH,)),
            dma((CHUNKS, PLANE)), dma((CHUNKS, PLANE)), dma((CHUNKS,)),
        ],
        compiler_params=pltpu.CompilerParams(
            collective_id=0, has_side_effects=True, vmem_limit_bytes=56 * 2 ** 20
        ),
        cost_estimate=pl.CostEstimate(
            flops=2 * head * quarter * tokens, bytes_accessed=2 ** 24, transcendentals=0
        ),
    )(mine, saved)


def body(grad_out, saved, block_route):
    devices = lax.axis_size("context")
    tok, width = grad_out.shape
    fits = devices == PLANE * DEPTH and tok == devices * 8
    if fits and width % (PLANE * CHUNKS * 128) == 0 and saved.shape[1] % (devices * 128) == 0:
        return fused_body(grad_out, saved, block_route)
    return grid_body(grad_out, saved, block_route)


def solution(mesh):
    return jax.shard_map(
        body,
        mesh=mesh,
        in_specs=(
            P(("groups", "context"), None),
            P(("groups", "context"), None),
            P("groups", None),
        ),
        out_specs=P(("groups", "context"), None),
        check_vma=False,
    )
```
